32 devices in a mesh: nodes: 8 (over z, y), rep: 4 (over x, core).
Axes of the slice: x: 2, y: 2, z: 4, core: 2. Of those that a mesh axis runs over, the one named last changes fastest.
Arguments:
- memory: float32 [4096, 512], P('nodes'), may hold values from -16 to 16
- last_tick: int32 [4096], P('nodes'), may hold values from 0 to 499
- src_local: int32 [4096], P(('nodes', 'rep')), may hold values from 0 to 511
- dst_owner: int32 [4096, 1], P(('nodes', 'rep')), may hold values from 0 to 7; in each aligned block of 128 rows (0 to 127, 128 to 255, ...) at most 32 rows name the same one
- dst_local: int32 [4096], P(('nodes', 'rep')), may hold values from 0 to 511
- event_tick: int32 [4096], P(('nodes', 'rep')), may hold values from 500 to 999
- nbr_owner: int32 [4096, 16, 1], P(('nodes', 'rep')), may hold values from 0 to 7; in each aligned block of 2048 rows (0 to 2047, 2048 to 4095, ..., all dimensions but the last counted through in order) at most 512 rows name the same one
- nbr_local: int32 [4096, 16], P(('nodes', 'rep')), may hold values from 0 to 511
- nbr_tick: int32 [4096, 16], P(('nodes', 'rep')), may hold values from 0 to 499
- freq: float32 [128], replicated, may hold values from 0.002 to 0.5
- phase: float32 [128], replicated, may hold values from -3.140625 to 3.140625
- w_message: bfloat16 [1152, 512], replicated, may hold values from -0.1875 to 0.1875
- gru_input: float32 [3, 512, 512], P(None, None, 'rep'), may hold values from -0.5 to 0.5
- gru_hidden: float32 [3, 512, 512], P(None, None, 'rep'), may hold values from -0.25 to 0.25
- gru_bias: float32 [4, 512], P(None, 'rep'), may hold values from -3 to 3
- w_query: bfloat16 [512, 512], replicated, may hold values from -1 to 1
- w_keyval_mem: bfloat16 [512, 1024], replicated, may hold values from -0.25 to 0.25
- w_keyval_time: bfloat16 [128, 1024], replicated, may hold values from -0.5 to 0.5
Outputs:
- new_memory: float32 [4096, 512], P('nodes', 'rep')
- embed: bfloat16 [4096, 512], P(('nodes', 'rep'))
The draws below stay inside these ranges and needn't reach their ends.
Inputs may be any that keep to these rules, and one draw needn't show every extreme that they name: `dst_owner`: on one device no owner is named by more than 32 events. `nbr_owner`: on one device no owner is named by more than 512 neighbour entries.
All inputs are finite; a program needn't handle non-finite values.
Results may differ from the reference program's by a relative error of at most 0.012.
The reference program's roundings to bfloat16 on the way (of `mem_half`, `upd_half`, `query` and `kv_mem`) count: a program that leaves them out, or rounds other values in their place, can miss the bound.
Values may be sent and summed in bfloat16 or wider, within the bound.
A program may use at most 128 MiB of HBM per device.

```python
import math
import jax
import jax.numpy as jnp
import numpy as np
from jax import lax

M = 512
MSG = 512
TE = 128
HEADS = 8
HEAD_DIM = 64
NBR = 16
EV_DEV = 128
ROWS_DEV = 512
E = 512
CAPD = 32
CAPN = 512
EVENTS = 4096
ROWS = 4096
N_NODES = 8
N_REP = 4


def draw_memory(key, part):
    first = jax.random.fold_in(jax.random.fold_in(key, 7), 0)
    base = jnp.clip(jax.random.normal(first, (ROWS, M), jnp.float32), -4.0, 4.0)
    return base


def place_ends(drawn, rng, low, high):
    extent = drawn.shape
    place = [jax.random.randint(jax.random.fold_in(rng, axis), (), 0, extent[axis]) for axis in range(len(extent))]
    drawn = drawn.at[tuple(place)].set(low)
    longest = extent.index(max(extent))
    place[longest] = (place[longest] + 1) % extent[longest]
    return drawn.at[tuple(place)].set(high)


def steps_of(rng, extent, shards, least, high):
    gain, own = 1.0, jax.random.fold_in(rng, 6)
    for dim, parts in shards:
        heights = jnp.exp(jax.random.uniform(jax.random.fold_in(own, dim), (parts,), jnp.float32, least / len(shards), high / len(shards)))
        gain = gain * jnp.repeat(heights, extent[dim] // parts).reshape([-1 if axis == dim else 1 for axis in range(len(extent))])
    return gain


def assign_block(key, own, number, rows, number_of, top, reach, skew):
    ranking = jax.random.permutation(key, number_of)
    heavy_load, common = portions_of(number_of, rows * top, reach, skew, True), portions_of(number_of, rows * top, reach, skew, False)
    places = jnp.arange(number_of)

    def named(lengths, offset_by):
        used = int((lengths > 0).sum())
        fixed = max(1, used // 4)
        passed = fixed + (places - fixed + offset_by * (used - fixed)) % max(1, number_of - fixed)
        return jnp.zeros((number_of,), jnp.int32).at[ranking[jnp.where(places < fixed, places, passed)]].set(jnp.asarray(lengths, jnp.int32))

    lengths = jnp.where(number % 4 == 0, named(heavy_load, number // 4), named(common, number - number // 4 - 1))
    mixed = jax.random.permutation(jax.random.fold_in(own, 3), number_of)
    source_of, sink = mixed[0:number_of // 2 * 2:2], mixed[1:number_of // 2 * 2:2]
    slack = jnp.minimum(lengths[source_of] - 1, reach - lengths[sink]) // 2
    slack = jnp.where((source_of == ranking[0]) | (sink == ranking[0]) | (lengths[sink] == 0), 0, jnp.maximum(slack, 0))
    passed = jax.random.randint(jax.random.fold_in(own, 4), (number_of // 2,), 0, 1 << 20) % (slack + 1)
    lengths = lengths.at[source_of].add(-passed).at[sink].add(passed)
    labels = jnp.searchsorted(jnp.cumsum(lengths), jnp.arange(rows * top), side="right").astype(jnp.int32)
    table = labels.reshape(top, rows).T
    table = table[jax.random.permutation(jax.random.fold_in(own, 1), rows)]
    offset_by = jax.random.randint(jax.random.fold_in(own, 2), (rows, 1), 0, top)
    return jnp.take_along_axis(table, (jnp.arange(top)[None, :] + offset_by) % top, axis=1)


def portions_of(amount, total, limit, lean, full):
    loads = [(1 << 20) // math.isqrt(standing ** lean) + 1 for standing in range(1, amount + 1)]
    largest = limit if full else min(limit, max(-(-total // amount), total * loads[0] // sum(loads)))
    least = 1 if total - largest >= amount - 1 else 0
    holding, spare = [largest] + [least] * (amount - 1), total - largest - least * (amount - 1)
    while spare > 0:
        candidates = [i for i in range(1, amount) if holding[i] < largest] or [i for i in range(1, amount) if holding[i] < limit]
        pool, remaining = sum([loads[i] for i in candidates]), spare
        for i in candidates:
            addition = min(limit - holding[i], max(1, remaining * loads[i] // pool), spare)
            holding[i] = holding[i] + addition
            spare = spare - addition
    return np.array(holding)


def normal_values(own_key, extent, width, limit, pieces=(), kind=jnp.bfloat16):
    drawn = jax.random.normal(own_key, extent, jnp.float32) * width
    if len(pieces) > 0:
        drawn = steps_of(own_key, extent, pieces, -0.22, 0.18) * drawn
    return jnp.clip(drawn, min=-limit, max=limit).astype(kind)


def setup_inputs(seed: int = 0) -> dict:
    arg_keys = jax.random.split(jax.random.key(seed), 19)
    memory = draw_memory(jax.random.fold_in(arg_keys[18], 71), 0)
    last_tick = place_ends(jax.random.randint(arg_keys[1], (ROWS,), 0, 500), jax.random.fold_in(arg_keys[1], 1), 0, 499).astype(jnp.int32)
    src_local = place_ends(jax.random.randint(arg_keys[2], (EVENTS,), 0, ROWS_DEV), jax.random.fold_in(arg_keys[2], 1), 0, ROWS_DEV - 1).astype(jnp.int32)
    dst_owner_keys = jax.random.split(jax.random.fold_in(arg_keys[3], 1), EVENTS // EV_DEV)
    dst_owner_turns = jax.random.permutation(jax.random.fold_in(arg_keys[3], 3), EVENTS // EV_DEV)
    dst_owner = jax.vmap(lambda own, number: assign_block(jax.random.fold_in(arg_keys[3], 2), own, number, EV_DEV, N_NODES, 1, CAPD, 2))(dst_owner_keys, dst_owner_turns).reshape((EVENTS, 1))
    dst_local = place_ends(jax.random.randint(arg_keys[4], (EVENTS,), 0, ROWS_DEV), jax.random.fold_in(arg_keys[4], 1), 0, ROWS_DEV - 1).astype(jnp.int32)
    event_tick = place_ends(jax.random.randint(arg_keys[5], (EVENTS,), 500, 1000), jax.random.fold_in(arg_keys[5], 1), 500, 999).astype(jnp.int32)
    nbr_owner_keys = jax.random.split(jax.random.fold_in(arg_keys[6], 1), EVENTS * NBR // (EV_DEV * NBR))
    nbr_owner_turns = jax.random.permutation(jax.random.fold_in(arg_keys[6], 3), EVENTS * NBR // (EV_DEV * NBR))
    nbr_owner = jax.vmap(lambda own, number: assign_block(jax.random.fold_in(arg_keys[6], 2), own, number, EV_DEV * NBR, N_NODES, 1, CAPN, 2))(nbr_owner_keys, nbr_owner_turns).reshape((EVENTS, NBR, 1))
    nbr_local = place_ends(jax.random.randint(arg_keys[7], (EVENTS, NBR), 0, ROWS_DEV), jax.random.fold_in(arg_keys[7], 1), 0, ROWS_DEV - 1).astype(jnp.int32)
    nbr_tick = place_ends(jax.random.randint(arg_keys[8], (EVENTS, NBR), 0, 500), jax.random.fold_in(arg_keys[8], 1), 0, 499).astype(jnp.int32)
    freq = jnp.clip(jnp.exp(jax.random.uniform(arg_keys[9], (TE,), jnp.float32, math.log(0.002), math.log(0.5))), 0.002, 0.5)
    phase = jnp.clip(jax.random.uniform(arg_keys[10], (TE,), jnp.float32, -3.140625, 3.140625), -3.140625, 3.140625)
    w_message = normal_values(arg_keys[11], (2 * M + TE, MSG), (2 * M + TE) ** -0.5, 0.1875)
    gru_input = normal_values(arg_keys[12], (3, MSG, M), (MSG // 4) ** -0.5, 0.5, ((2, 4),), jnp.float32)
    gru_hidden = normal_values(arg_keys[13], (3, M, M), M ** -0.5, 0.25, ((2, 4),), jnp.float32)
    gru_bias = normal_values(arg_keys[14], (4, M), 0.5, 3.0, ((1, 4),), jnp.float32)
    w_query = normal_values(arg_keys[15], (M, E), (M // 16) ** -0.5, 1.0)
    w_keyval_mem = normal_values(arg_keys[16], (M, 2 * E), M ** -0.5, 0.25)
    w_keyval_time = normal_values(arg_keys[17], (TE, 2 * E), TE ** -0.5, 0.5)
    return dict(memory=memory, last_tick=last_tick, src_local=src_local, dst_owner=dst_owner, dst_local=dst_local, event_tick=event_tick, nbr_owner=nbr_owner, nbr_local=nbr_local, nbr_tick=nbr_tick, freq=freq, phase=phase, w_message=w_message, gru_input=gru_input, gru_hidden=gru_hidden, gru_bias=gru_bias, w_query=w_query, w_keyval_mem=w_keyval_mem, w_keyval_time=w_keyval_time)


def encode(gaps, freq, phase):
    return jnp.cos(gaps[..., None] * freq + phase)

def reference(memory, last_tick, src_local, dst_owner, dst_local, event_tick, nbr_owner, nbr_local, nbr_tick, freq, phase, w_message, gru_input, gru_hidden, gru_bias, w_query, w_keyval_mem, w_keyval_time):
    events = src_local.shape[0]
    total_rows = memory.shape[0]
    group = jnp.arange(events, dtype=jnp.int32) // (EV_DEV * N_REP)
    source = (group * ROWS_DEV + src_local).astype(jnp.int32)
    target = (dst_owner[:, 0] * ROWS_DEV + dst_local).astype(jnp.int32)
    mem_half = memory.astype(jnp.bfloat16)
    ticks = event_tick.astype(jnp.float32)
    src_time = encode(ticks - last_tick[source].astype(jnp.float32), freq, phase).astype(jnp.bfloat16)
    dst_time = encode(ticks - last_tick[target].astype(jnp.float32), freq, phase).astype(jnp.bfloat16)
    src_in = jnp.concatenate([mem_half[source], mem_half[target], src_time], axis=1)
    dst_in = jnp.concatenate([mem_half[target], mem_half[source], dst_time], axis=1)
    msg_src = jax.nn.silu(jnp.dot(src_in, w_message, preferred_element_type=jnp.float32)).astype(jnp.bfloat16)
    msg_dst = jax.nn.silu(jnp.dot(dst_in, w_message, preferred_element_type=jnp.float32)).astype(jnp.bfloat16)
    msg_src = lax.optimization_barrier(msg_src).astype(jnp.float32)
    msg_dst = lax.optimization_barrier(msg_dst).astype(jnp.float32)
    sums = jax.ops.segment_sum(msg_src, source, total_rows) + jax.ops.segment_sum(msg_dst, target, total_rows)
    ones = jnp.ones((events,), jnp.float32)
    counts = jax.ops.segment_sum(ones, source, total_rows) + jax.ops.segment_sum(ones, target, total_rows)
    mean = sums / jnp.maximum(counts, 1.0)[:, None]
    highest = lax.Precision.HIGHEST
    a_parts = [jnp.dot(mean, gru_input[g], precision=highest) for g in range(3)]
    b_parts = [jnp.dot(memory, gru_hidden[g], precision=highest) for g in range(3)]
    update = jax.nn.sigmoid(a_parts[0] + b_parts[0] + gru_bias[0])
    reset = jax.nn.sigmoid(a_parts[1] + b_parts[1] + gru_bias[1])
    cand = jnp.tanh(a_parts[2] + gru_bias[2] + reset * (b_parts[2] + gru_bias[3]))
    fresh = (1.0 - update) * cand + update * memory
    new_memory = jnp.where((counts > 0.0)[:, None], fresh, memory)
    upd_half = new_memory.astype(jnp.bfloat16)
    query = jnp.dot(upd_half[source], w_query, preferred_element_type=jnp.float32).astype(jnp.bfloat16)
    query = lax.optimization_barrier(query).astype(jnp.float32)
    blocks = events // EV_DEV
    attn_width = HEADS * HEAD_DIM

    def attend(inputs):
        q_block, own_block, loc_block, ntick_block, tick_block = inputs
        nbr = (own_block[:, :, 0] * ROWS_DEV + loc_block).astype(jnp.int32)
        rows_block = upd_half[nbr.reshape(-1)]
        kv_mem = jnp.dot(rows_block, w_keyval_mem, preferred_element_type=jnp.float32).astype(jnp.bfloat16)
        kv_mem = lax.optimization_barrier(kv_mem).astype(jnp.float32)
        gaps = tick_block.astype(jnp.float32)[:, None] - ntick_block.astype(jnp.float32)
        time_enc = encode(gaps, freq, phase).reshape(-1, freq.shape[0]).astype(jnp.bfloat16)
        kv_time = jnp.dot(time_enc, w_keyval_time, preferred_element_type=jnp.float32)
        keyval = (kv_mem + kv_time).reshape(EV_DEV, NBR, 2, HEADS, HEAD_DIM)
        qh = q_block.reshape(EV_DEV, HEADS, HEAD_DIM)
        scores = jnp.einsum('ehd,ejhd->ehj', qh, keyval[:, :, 0]) / math.sqrt(HEAD_DIM)
        weights = jax.nn.softmax(scores, axis=-1)
        out = jnp.einsum('ehj,ejhd->ehd', weights, keyval[:, :, 1])
        return out.reshape(EV_DEV, attn_width).astype(jnp.bfloat16)
    embed = lax.map(attend, (query.reshape(blocks, EV_DEV, attn_width), nbr_owner.reshape(blocks, EV_DEV, NBR, 1), nbr_local.reshape(blocks, EV_DEV, NBR), nbr_tick.reshape(blocks, EV_DEV, NBR), event_tick.reshape(blocks, EV_DEV)))
    return (new_memory, embed.reshape(events, attn_width))
```

```python
import functools
import math

import jax
import jax.numpy as jnp
from jax import lax
from jax.experimental import pallas as pl
from jax.experimental.pallas import tpu as pltpu
from jax.sharding import PartitionSpec as P

HEADS = 8
HEAD_DIM = 64
MESH = pl.DeviceIdType.MESH
F32 = jnp.float32
BF16 = jnp.bfloat16


def dot32(a, b):
    return jnp.dot(a, b, preferred_element_type=F32)


def split(v):
    high = v.astype(BF16)
    return high, (v - high.astype(F32)).astype(BF16)


def column(ref, j, count):
    lanes = lax.broadcasted_iota(jnp.int32, ref.shape, 1)
    value = ref[...]
    cols = [
        jnp.sum(jnp.where(lanes == j + i, value, 0.0), axis=1, keepdims=True) for i in range(count)
    ]
    return jnp.concatenate(cols, axis=0)


def attend_kernel(
    groups,
    part_ref,
    src_ref,
    index_ref,
    gap_ref,
    freq_ref,
    phase_ref,
    wq_ref,
    wkv_ref,
    wt_ref,
    out_ref,
    table,
    keyval,
    scores,
    send_z,
    recv_z,
    send_a,
    recv_a,
    send_b,
    recv_b,
    send_c,
    recv_c,
):
    node = lax.axis_index("nodes")
    rep = lax.axis_index("rep")
    deep = groups // 2
    z, y = node // 2, node % 2
    x, c = rep // 2, rep % 2
    rows, unit = part_ref.shape
    half = rows // 2
    events, neighbours = index_ref.shape
    width = table.shape[1]

    def where_of(h, d, k, b):
        zz = (z + deep - d) % deep
        ky, kx = (k, b) if h == 0 else (b, k)
        return zz * 2 + (y + ky) % 2, (x + kx) % 2

    def block(n, r, h):
        return table.at[
            pl.ds(pl.multiple_of(n * rows + h * half, half), half),
            pl.ds(pl.multiple_of(r * unit, unit), unit),
        ]

    def copy(n, r, h, device, send, recv):
        return pltpu.make_async_remote_copy(
            src_ref=block(n, r, h),
            dst_ref=block(n, r, h),
            send_sem=send,
            recv_sem=recv,
            device_id=device,
            device_id_type=MESH,
        )

    across_y = (z * 2 + (y + 1) % 2, rep)
    across_x = (node, ((x + 1) % 2) * 2 + c)
    across_c = (node, x * 2 + (c + 1) % 2)

    def along_z(h, d):
        device = (((z + d) % deep) * 2 + y, rep)
        return copy(node, rep, h, device, send_z.at[h, d], recv_z.at[h, d])

    def first(h, d):
        n, xx = where_of(h, d, 0, 0)
        device = across_y if h == 0 else across_x
        return copy(n, xx * 2 + c, h, device, send_a.at[h, d], recv_a.at[h, d])

    def second(h, d, k):
        n, xx = where_of(h, d, k, 0)
        device = across_x if h == 0 else across_y
        return copy(n, xx * 2 + c, h, device, send_b.at[h, d, k], recv_b.at[h, d, k])

    def core(h, d, k, b):
        n, xx = where_of(h, d, k, b)
        i = k * 2 + b
        return copy(n, xx * 2 + c, h, across_c, send_c.at[h, d, i], recv_c.at[h, d, i])

    block_rows = pl.ds(pl.multiple_of(node * rows, rows), rows)
    table[block_rows, pl.ds(pl.multiple_of(rep * unit, unit), unit)] = part_ref[...]

    partners = [(((z + d) % deep) * 2 + y, rep) for d in range(1, deep)]
    partners += [across_y, across_x, across_c]
    barrier = pltpu.get_barrier_semaphore()
    for device in partners:
        pl.semaphore_signal(barrier, inc=1, device_id=device, device_id_type=MESH)
    pl.semaphore_wait(barrier, len(partners))

    started = []

    def start(one):
        one.start()
        started.append(one)

    batch = 4

    def time_part(g):
        gaps = column(gap_ref, g * batch, batch)
        enc = jnp.cos(gaps * freq_ref[...] + phase_ref[...]).astype(BF16)
        size = batch * events
        keyval[g * size : (g + 1) * size, :] = dot32(enc, wt_ref[...])

    steps = neighbours // batch
    for d in range(1, deep):
        for h in range(2):
            start(along_z(h, d))
    for h in range(2):
        start(first(h, 0))
        start(second(h, 0, 0))
        start(core(h, 0, 0, 0))
    time_part(0)
    for d in range(1, deep):
        for h in range(2):
            along_z(h, d).wait_recv()
            start(first(h, d))
            start(second(h, d, 0))
            start(core(h, d, 0, 0))
        if d < steps:
            time_part(d)
    for g in range(deep, steps):
        time_part(g)
    for d in range(deep):
        for h in range(2):
            first(h, d).wait_recv()
            start(second(h, d, 1))
            start(core(h, d, 1, 0))
    for d in range(deep):
        for k in range(2):
            for h in range(2):
                second(h, d, k).wait_recv()
                start(core(h, d, k, 1))
    for d in range(deep):
        for k in range(2):
            for b in range(2):
                for h in range(2):
                    core(h, d, k, b).wait_recv()
    for one in started:
        one.wait_send()

    lane_row = lax.broadcasted_iota(jnp.int32, (events, rows), 1)
    hit = (src_ref[...] == lane_row).astype(BF16)
    mine = dot32(hit, table[block_rows, :]).astype(BF16)
    query = dot32(mine, wq_ref[...]).astype(BF16).astype(F32) * (1.0 / math.sqrt(HEAD_DIM))
    query = jnp.concatenate([query] * batch, axis=0)
    att = HEADS * HEAD_DIM
    size = batch * events
    head_sum = (
        lax.broadcasted_iota(jnp.int32, (att, 128), 0) // HEAD_DIM
        == lax.broadcasted_iota(jnp.int32, (att, 128), 1)
    ).astype(BF16)
    head_spread = (
        lax.broadcasted_iota(jnp.int32, (128, att), 1) // HEAD_DIM
        == lax.broadcasted_iota(jnp.int32, (128, att), 0)
    ).astype(BF16)
    lanes = lax.broadcasted_iota(jnp.int32, (size, rows), 1)

    @pl.loop(0, steps)
    def _(g):
        names = column(index_ref, g * batch, batch).astype(jnp.int32)
        here = pl.ds(pl.multiple_of(g * size, size), size)
        found = jnp.zeros((size, width), F32)
        for n in range(groups):
            chosen = (names == lanes + n * rows).astype(BF16)
            found += dot32(chosen, table[n * rows : (n + 1) * rows, :])
        kv = dot32(found.astype(BF16), wkv_ref[...]).astype(BF16).astype(F32)
        kv = kv + keyval[here, :]
        keyval[here, att:] = kv[:, att:]
        high, low = split(query * kv[:, :att])
        scores[here, :] = dot32(high, head_sum) + dot32(low, head_sum)

    top = scores[0:events, :]
    for j in range(1, neighbours):
        top = jnp.maximum(top, scores[j * events : (j + 1) * events, :])
    total = jnp.zeros_like(top)
    for j in range(neighbours):
        term = jnp.exp(scores[j * events : (j + 1) * events, :] - top)
        scores[j * events : (j + 1) * events, :] = term
        total += term
    mixed = jnp.zeros((events, att), F32)
    for g in range(steps):
        high, low = split(scores[g * size : (g + 1) * size, :])
        spread = dot32(high, head_spread) + dot32(low, head_spread)
        terms = spread * keyval[g * size : (g + 1) * size, att:]
        for i in range(batch):
            mixed += terms[i * events : (i + 1) * events, :]
    high, low = split(1.0 / total)
    scale = dot32(high, head_spread) + dot32(low, head_spread)
    out_ref[...] = (mixed * scale).astype(out_ref.dtype)


def attend(part, src, index, gaps, freq, phase, wq, wkv, wt, groups, reps):
    rows, unit = part.shape
    events, neighbours = index.shape
    deep = groups // 2
    total = groups * rows
    dma = pltpu.SemaphoreType.DMA
    pairs = [(2, deep), (2, deep), (2, deep, 2), (2, deep, 4)]
    sems = [dma(shape) for shape in pairs for _ in range(2)]
    return pl.pallas_call(
        functools.partial(attend_kernel, groups),
        out_shape=jax.ShapeDtypeStruct((events, HEADS * HEAD_DIM), BF16),
        in_specs=[pl.BlockSpec(memory_space=pltpu.VMEM)] * 9,
        out_specs=pl.BlockSpec(memory_space=pltpu.VMEM),
        scratch_shapes=[
            pltpu.VMEM((total, reps * unit), BF16),
            pltpu.VMEM((events * neighbours, wkv.shape[1]), F32),
            pltpu.VMEM((events * neighbours, 128), F32),
        ]
        + sems,
        compiler_params=pltpu.CompilerParams(
            collective_id=1, has_side_effects=True, vmem_limit_bytes=50 * 1024 * 1024
        ),
    )(part, src, index, gaps, freq, phase, wq, wkv, wt)


def encode(gaps, freq, phase):
    return jnp.cos(gaps[..., None] * freq + phase)


def place(owner, groups, capacity):
    onehot = (owner[:, None] == jnp.arange(groups, dtype=jnp.int32)[None, :]).astype(jnp.int32)
    before = jnp.cumsum(onehot, axis=0) - onehot
    return owner * capacity + jnp.sum(before * onehot, axis=1)


def message_pair(src_rows, dst_rows, src_time, dst_time, w_message):
    count = src_rows.shape[0]
    stacked = jnp.concatenate(
        [
            jnp.concatenate([src_rows, dst_rows, src_time], axis=1),
            jnp.concatenate([dst_rows, src_rows, dst_time], axis=1),
        ],
        axis=0,
    )
    messages = jax.nn.silu(jnp.dot(stacked, w_message, preferred_element_type=jnp.float32)).astype(
        jnp.bfloat16
    )
    return (messages[:count], messages[count:])


def on_device_large(
    memory,
    last_tick,
    src_local,
    dst_owner,
    dst_local,
    event_tick,
    nbr_owner,
    nbr_local,
    nbr_tick,
    freq,
    phase,
    w_message,
    gru_input,
    gru_hidden,
    gru_bias,
    w_query,
    w_keyval_mem,
    w_keyval_time,
):
    groups = lax.axis_size("nodes")
    events = src_local.shape[0]
    rows_here = memory.shape[0]
    width_m = memory.shape[1]
    neighbours = nbr_local.shape[1]
    msg_width = w_message.shape[1]
    dst_cap = max(2, 2 * events // groups)
    nbr_cap = 2 * events * neighbours // groups
    dst_slot = place(dst_owner[:, 0], groups, dst_cap)
    nbr_slot = place(nbr_owner.reshape(-1), groups, nbr_cap)
    dst_ids = (
        jnp.full((groups * dst_cap,), -1, jnp.int32)
        .at[dst_slot]
        .set(dst_local)
        .reshape(groups, dst_cap)
    )
    nbr_ids = (
        jnp.full((groups * nbr_cap,), -1, jnp.int32)
        .at[nbr_slot]
        .set(nbr_local.reshape(-1))
        .reshape(groups, nbr_cap)
    )
    mem_half = memory.astype(jnp.bfloat16)
    near_rows = mem_half[src_local]
    near_ticks = last_tick[src_local]
    ticks = event_tick.astype(jnp.float32)
    got_dst, got_nbr = (
        lax.all_to_all(dst_ids, "nodes", split_axis=0, concat_axis=0, tiled=True),
        lax.all_to_all(nbr_ids, "nodes", split_axis=0, concat_axis=0, tiled=True),
    )
    safe_dst = jnp.maximum(got_dst, 0)
    reply_rows, reply_ticks = (
        lax.all_to_all(mem_half[safe_dst], "nodes", split_axis=0, concat_axis=0, tiled=True),
        lax.all_to_all(last_tick[safe_dst], "nodes", split_axis=0, concat_axis=0, tiled=True),
    )
    far_rows = reply_rows.reshape(-1, width_m)[dst_slot]
    far_ticks = reply_ticks.reshape(-1)[dst_slot]
    src_time = encode(ticks - near_ticks.astype(jnp.float32), freq, phase).astype(jnp.bfloat16)
    dst_time = encode(ticks - far_ticks.astype(jnp.float32), freq, phase).astype(jnp.bfloat16)
    msg_src, msg_dst = message_pair(near_rows, far_rows, src_time, dst_time, w_message)
    outgoing = (
        jnp.zeros((groups * dst_cap, msg_width), jnp.bfloat16)
        .at[dst_slot]
        .set(msg_dst)
        .reshape(groups, dst_cap, msg_width)
    )
    incoming = lax.all_to_all(outgoing, "nodes", split_axis=0, concat_axis=0, tiled=True)
    far_msgs = incoming.reshape(-1, msg_width)
    row_ids = jnp.arange(rows_here, dtype=jnp.int32)[:, None]
    hit_far = (row_ids == got_dst.reshape(1, -1)).astype(jnp.bfloat16)
    hit_near = (row_ids == src_local[None, :]).astype(jnp.bfloat16)
    sums = jnp.dot(hit_near, msg_src, preferred_element_type=jnp.float32) + jnp.dot(
        hit_far, far_msgs, preferred_element_type=jnp.float32
    )
    counts = jnp.sum(hit_near.astype(jnp.float32), axis=1) + jnp.sum(
        hit_far.astype(jnp.float32), axis=1
    )
    sums, counts = lax.psum((sums, counts), "rep")
    unit_width = gru_bias.shape[1]
    start = lax.axis_index("rep") * unit_width
    state_part = lax.dynamic_slice_in_dim(memory, start, unit_width, 1)
    mean = sums / jnp.maximum(counts, 1.0)[:, None]
    highest = lax.Precision.HIGHEST
    a_parts = jnp.einsum("rk,gku->gru", mean, gru_input, precision=highest)
    b_parts = jnp.einsum("rk,gku->gru", memory, gru_hidden, precision=highest)
    update = jax.nn.sigmoid(a_parts[0] + b_parts[0] + gru_bias[0])
    reset = jax.nn.sigmoid(a_parts[1] + b_parts[1] + gru_bias[1])
    cand = jnp.tanh(a_parts[2] + gru_bias[2] + reset * (b_parts[2] + gru_bias[3]))
    fresh = (1.0 - update) * cand + update * state_part
    new_part = jnp.where((counts > 0.0)[:, None], fresh, state_part)
    updated = lax.all_gather(new_part.astype(jnp.bfloat16), "rep", axis=1, tiled=True)
    served = updated[jnp.maximum(got_nbr, 0)]
    returned = lax.all_to_all(served, "nodes", split_axis=0, concat_axis=0, tiled=True)
    fetched = returned.reshape(-1, updated.shape[1])[nbr_slot]
    kv_mem = jnp.dot(fetched, w_keyval_mem, preferred_element_type=jnp.float32).astype(jnp.bfloat16)
    kv_mem = lax.optimization_barrier(kv_mem).astype(jnp.float32)
    gaps = ticks[:, None] - nbr_tick.astype(jnp.float32)
    time_enc = encode(gaps, freq, phase).reshape(-1, freq.shape[0]).astype(jnp.bfloat16)
    kv_time = jnp.dot(time_enc, w_keyval_time, preferred_element_type=jnp.float32)
    keyval = (kv_mem + kv_time).reshape(events, neighbours, 2, HEADS, HEAD_DIM)
    query = jnp.dot(updated[src_local], w_query, preferred_element_type=jnp.float32).astype(
        jnp.bfloat16
    )
    query = lax.optimization_barrier(query).astype(jnp.float32).reshape(events, HEADS, HEAD_DIM)
    scores = jnp.einsum("ehd,ejhd->ehj", query, keyval[:, :, 0]) / math.sqrt(HEAD_DIM)
    weights = jax.nn.softmax(scores, axis=-1)
    mixed = jnp.einsum("ehj,ejhd->ehd", weights, keyval[:, :, 1])
    embed = mixed.reshape(events, HEADS * HEAD_DIM).astype(jnp.bfloat16)
    return (new_part, embed)


def on_device(
    memory,
    last_tick,
    src_local,
    dst_owner,
    dst_local,
    event_tick,
    nbr_owner,
    nbr_local,
    nbr_tick,
    freq,
    phase,
    w_message,
    gru_input,
    gru_hidden,
    gru_bias,
    w_query,
    w_keyval_mem,
    w_keyval_time,
):
    groups = lax.axis_size("nodes")
    events = src_local.shape[0]
    rows_here = memory.shape[0]
    width_m = memory.shape[1]
    msg_width = w_message.shape[1]
    dst_cap = max(2, 2 * events // groups)
    dst_slot = place(dst_owner[:, 0], groups, dst_cap)
    dst_ids = (
        jnp.full((groups * dst_cap,), -1, jnp.int32)
        .at[dst_slot]
        .set(dst_local)
        .reshape(groups, dst_cap)
    )
    mem_half = memory.astype(jnp.bfloat16)
    near_rows = mem_half[src_local]
    near_ticks = last_tick[src_local]
    ticks = event_tick.astype(jnp.float32)
    got_dst = lax.all_to_all(dst_ids, "nodes", split_axis=0, concat_axis=0, tiled=True)
    names = jnp.concatenate([src_local, got_dst.reshape(-1)])
    names = lax.all_gather(names, "rep", axis=0, tiled=True)
    safe_dst = jnp.maximum(got_dst, 0)
    reply_rows, reply_ticks = (
        lax.all_to_all(mem_half[safe_dst], "nodes", split_axis=0, concat_axis=0, tiled=True),
        lax.all_to_all(last_tick[safe_dst], "nodes", split_axis=0, concat_axis=0, tiled=True),
    )
    far_rows = reply_rows.reshape(-1, width_m)[dst_slot]
    far_ticks = reply_ticks.reshape(-1)[dst_slot]
    src_time = encode(ticks - near_ticks.astype(jnp.float32), freq, phase).astype(jnp.bfloat16)
    dst_time = encode(ticks - far_ticks.astype(jnp.float32), freq, phase).astype(jnp.bfloat16)
    msg_src, msg_dst = message_pair(near_rows, far_rows, src_time, dst_time, w_message)
    outgoing = (
        jnp.zeros((groups * dst_cap, msg_width), jnp.bfloat16)
        .at[dst_slot]
        .set(msg_dst)
        .reshape(groups, dst_cap, msg_width)
    )
    incoming = lax.all_to_all(outgoing, "nodes", split_axis=0, concat_axis=0, tiled=True)
    far_msgs = incoming.reshape(-1, msg_width)
    row_ids = jnp.arange(rows_here, dtype=jnp.int32)[:, None]
    messages = jnp.concatenate([msg_src, far_msgs], axis=0)
    messages = lax.all_gather(messages, "rep", axis=0, tiled=True)
    hits = (row_ids == names[None, :]).astype(jnp.bfloat16)
    sums = jnp.dot(hits, messages, preferred_element_type=jnp.float32)
    counts = jnp.sum(hits.astype(jnp.float32), axis=1)
    unit_width = gru_bias.shape[1]
    start = lax.axis_index("rep") * unit_width
    state_part = lax.dynamic_slice_in_dim(memory, start, unit_width, 1)
    mean = sums / jnp.maximum(counts, 1.0)[:, None]
    highest = lax.Precision.HIGHEST
    a_parts = jnp.einsum("rk,gku->gru", mean, gru_input, precision=highest)
    b_parts = jnp.einsum("rk,gku->gru", memory, gru_hidden, precision=highest)
    update = jax.nn.sigmoid(a_parts[0] + b_parts[0] + gru_bias[0])
    reset = jax.nn.sigmoid(a_parts[1] + b_parts[1] + gru_bias[1])
    cand = jnp.tanh(a_parts[2] + gru_bias[2] + reset * (b_parts[2] + gru_bias[3]))
    fresh = (1.0 - update) * cand + update * state_part
    new_part = jnp.where((counts > 0.0)[:, None], fresh, state_part)
    index = (nbr_owner[:, :, 0] * rows_here + nbr_local).astype(jnp.float32)
    gaps = ticks[:, None] - nbr_tick.astype(jnp.float32)
    embed = attend(
        new_part.astype(jnp.bfloat16),
        src_local[:, None],
        index,
        gaps,
        freq[None, :],
        phase[None, :],
        w_query,
        w_keyval_mem,
        w_keyval_time,
        groups,
        lax.axis_size("rep"),
    )
    return (new_part, embed)


def solution(mesh):
    placed = (
        P("nodes", None),
        P("nodes"),
        P(("nodes", "rep")),
        P(("nodes", "rep"), None),
        P(("nodes", "rep")),
        P(("nodes", "rep")),
        P(("nodes", "rep"), None, None),
        P(("nodes", "rep"), None),
        P(("nodes", "rep"), None),
        P(),
        P(),
        P(),
        P(None, None, "rep"),
        P(None, None, "rep"),
        P(None, "rep"),
        P(),
        P(),
        P(),
    )
    fits = mesh.shape["nodes"] == 8 and mesh.shape["rep"] == 4
    return jax.shard_map(
        on_device if fits else on_device_large,
        mesh=mesh,
        in_specs=placed,
        out_specs=(P("nodes", "rep"), P(("nodes", "rep"), None)),
        check_vma=False,
    )
```

```python
import functools
import math

import jax
import jax.numpy as jnp
from jax import lax
from jax.experimental import pallas as pl
from jax.experimental.pallas import tpu as pltpu
from jax.sharding import PartitionSpec as P

HEADS = 8
HEAD_DIM = 64
MESH = pl.DeviceIdType.MESH
F32 = jnp.float32
BF16 = jnp.bfloat16


def dot32(a, b):
    return jnp.dot(a, b, preferred_element_type=F32)


def split(v):
    high = v.astype(BF16)
    return high, (v - high.astype(F32)).astype(BF16)


def column(ref, j, count):
    lanes = lax.broadcasted_iota(jnp.int32, ref.shape, 1)
    value = ref[...]
    cols = [
        jnp.sum(jnp.where(lanes == j + i, value, 0.0), axis=1, keepdims=True) for i in range(count)
    ]
    return jnp.concatenate(cols, axis=0)


def attend_kernel(
    groups,
    part_ref,
    src_ref,
    index_ref,
    gap_ref,
    freq_ref,
    phase_ref,
    wq_ref,
    wkv_ref,
    wt_ref,
    out_ref,
    table,
    keyval,
    scores,
    send_z,
    recv_z,
    send_a,
    recv_a,
    send_b,
    recv_b,
    send_c,
    recv_c,
):
    node = lax.axis_index("nodes")
    rep = lax.axis_index("rep")
    deep = groups // 2
    z, y = node // 2, node % 2
    x, c = rep // 2, rep % 2
    rows, unit = part_ref.shape
    half = rows // 2
    events, neighbours = index_ref.shape
    width = table.shape[1]

    def where_of(h, d, k, b):
        zz = (z + deep - d) % deep
        ky, kx = (k, b) if h == 0 else (b, k)
        return zz * 2 + (y + ky) % 2, (x + kx) % 2

    def block(n, r, h):
        return table.at[
            pl.ds(pl.multiple_of(n * rows + h * half, half), half),
            pl.ds(pl.multiple_of(r * unit, unit), unit),
        ]

    def copy(n, r, h, device, send, recv):
        return pltpu.make_async_remote_copy(
            src_ref=block(n, r, h),
            dst_ref=block(n, r, h),
            send_sem=send,
            recv_sem=recv,
            device_id=device,
            device_id_type=MESH,
        )

    across_y = (z * 2 + (y + 1) % 2, rep)
    across_x = (node, ((x + 1) % 2) * 2 + c)
    across_c = (node, x * 2 + (c + 1) % 2)

    def along_z(h, d):
        device = (((z + d) % deep) * 2 + y, rep)
        return copy(node, rep, h, device, send_z.at[h, d], recv_z.at[h, d])

    def first(h, d):
        n, xx = where_of(h, d, 0, 0)
        device = across_y if h == 0 else across_x
        return copy(n, xx * 2 + c, h, device, send_a.at[h, d], recv_a.at[h, d])

    def second(h, d, k):
        n, xx = where_of(h, d, k, 0)
        device = across_x if h == 0 else across_y
        return copy(n, xx * 2 + c, h, device, send_b.at[h, d, k], recv_b.at[h, d, k])

    def core(h, d, k, b):
        n, xx = where_of(h, d, k, b)
        i = k * 2 + b
        return copy(n, xx * 2 + c, h, across_c, send_c.at[h, d, i], recv_c.at[h, d, i])

    block_rows = pl.ds(pl.multiple_of(node * rows, rows), rows)
    table[block_rows, pl.ds(pl.multiple_of(rep * unit, unit), unit)] = part_ref[...]

    partners = [(((z + d) % deep) * 2 + y, rep) for d in range(1, deep)]
    partners += [across_y, across_x, across_c]
    barrier = pltpu.get_barrier_semaphore()
    for device in partners:
        pl.semaphore_signal(barrier, inc=1, device_id=device, device_id_type=MESH)
    pl.semaphore_wait(barrier, len(partners))

    started = []

    def start(one):
        one.start()
        started.append(one)

    batch = 4

    def time_part(g):
        gaps = column(gap_ref, g * batch, batch)
        enc = jnp.cos(gaps * freq_ref[...] + phase_ref[...]).astype(BF16)
        size = batch * events
        keyval[g * size : (g + 1) * size, :] = dot32(enc, wt_ref[...])

    steps = neighbours // batch
    for d in range(1, deep):
        for h in range(2):
            start(along_z(h, d))
    for h in range(2):
        start(first(h, 0))
        start(second(h, 0, 0))
        start(core(h, 0, 0, 0))
    time_part(0)
    for d in range(1, deep):
        for h in range(2):
            along_z(h, d).wait_recv()
            start(first(h, d))
            start(second(h, d, 0))
            start(core(h, d, 0, 0))
        if d < steps:
            time_part(d)
    for g in range(deep, steps):
        time_part(g)
    for d in range(deep):
        for h in range(2):
            first(h, d).wait_recv()
            start(second(h, d, 1))
            start(core(h, d, 1, 0))
    for d in range(deep):
        for k in range(2):
            for h in range(2):
                second(h, d, k).wait_recv()
                start(core(h, d, k, 1))
    for d in range(deep):
        for k in range(2):
            for b in range(2):
                for h in range(2):
                    core(h, d, k, b).wait_recv()
    for one in started:
        one.wait_send()

    lane_row = lax.broadcasted_iota(jnp.int32, (events, rows), 1)
    hit = (src_ref[...] == lane_row).astype(BF16)
    mine = dot32(hit, table[block_rows, :]).astype(BF16)
    query = dot32(mine, wq_ref[...]).astype(BF16).astype(F32) * (1.0 / math.sqrt(HEAD_DIM))
    query = jnp.concatenate([query] * batch, axis=0)
    att = HEADS * HEAD_DIM
    size = batch * events
    head_sum = (
        lax.broadcasted_iota(jnp.int32, (att, 128), 0) // HEAD_DIM
        == lax.broadcasted_iota(jnp.int32, (att, 128), 1)
    ).astype(BF16)
    head_spread = (
        lax.broadcasted_iota(jnp.int32, (128, att), 1) // HEAD_DIM
        == lax.broadcasted_iota(jnp.int32, (128, att), 0)
    ).astype(BF16)
    lanes = lax.broadcasted_iota(jnp.int32, (size, rows), 1)

    @pl.loop(0, steps)
    def _(g):
        names = column(index_ref, g * batch, batch).astype(jnp.int32)
        here = pl.ds(pl.multiple_of(g * size, size), size)
        found = jnp.zeros((size, width), F32)
        for n in range(groups):
            chosen = (names == lanes + n * rows).astype(BF16)
            found += dot32(chosen, table[n * rows : (n + 1) * rows, :])
        kv = dot32(found.astype(BF16), wkv_ref[...]).astype(BF16).astype(F32)
        kv = kv + keyval[here, :]
        keyval[here, att:] = kv[:, att:]
        high, low = split(query * kv[:, :att])
        scores[here, :] = dot32(high, head_sum) + dot32(low, head_sum)

    top = scores[0:events, :]
    for j in range(1, neighbours):
        top = jnp.maximum(top, scores[j * events : (j + 1) * events, :])
    total = jnp.zeros_like(top)
    for j in range(neighbours):
        term = jnp.exp(scores[j * events : (j + 1) * events, :] - top)
        scores[j * events : (j + 1) * events, :] = term
        total += term
    mixed = jnp.zeros((events, att), F32)
    for g in range(steps):
        high, low = split(scores[g * size : (g + 1) * size, :])
        spread = dot32(high, head_spread) + dot32(low, head_spread)
        terms = spread * keyval[g * size : (g + 1) * size, att:]
        for i in range(batch):
            mixed += terms[i * events : (i + 1) * events, :]
    high, low = split(1.0 / total)
    scale = dot32(high, head_spread) + dot32(low, head_spread)
    out_ref[...] = (mixed * scale).astype(out_ref.dtype)


def attend(part, src, index, gaps, freq, phase, wq, wkv, wt, groups, reps):
    rows, unit = part.shape
    events, neighbours = index.shape
    deep = groups // 2
    total = groups * rows
    dma = pltpu.SemaphoreType.DMA
    pairs = [(2, deep), (2, deep), (2, deep, 2), (2, deep, 4)]
    sems = [dma(shape) for shape in pairs for _ in range(2)]
    return pl.pallas_call(
        functools.partial(attend_kernel, groups),
        out_shape=jax.ShapeDtypeStruct((events, HEADS * HEAD_DIM), BF16),
        in_specs=[pl.BlockSpec(memory_space=pltpu.VMEM)] * 9,
        out_specs=pl.BlockSpec(memory_space=pltpu.VMEM),
        scratch_shapes=[
            pltpu.VMEM((total, reps * unit), BF16),
            pltpu.VMEM((events * neighbours, wkv.shape[1]), F32),
            pltpu.VMEM((events * neighbours, 128), F32),
        ]
        + sems,
        compiler_params=pltpu.CompilerParams(
            collective_id=1, has_side_effects=True, vmem_limit_bytes=50 * 1024 * 1024
        ),
    )(part, src, index, gaps, freq, phase, wq, wkv, wt)


def dot_rows(a, b):
    return lax.dot_general(a, b, (((0,), (0,)), ((), ())), preferred_element_type=F32)


def three_pass(a, b_high, b_low):
    high, low = split(a)
    return dot32(high, b_high) + dot32(low, b_high) + dot32(high, b_low)


def silu(v):
    return v / (1.0 + jnp.exp(-v))


def sigmoid(v):
    return 1.0 / (1.0 + jnp.exp(-v))


def update_kernel(
    groups,
    memory_ref,
    tick_ref,
    cols_ref,
    src_ref,
    freq_ref,
    phase_ref,
    wm_ref,
    wi_ref,
    wh_ref,
    bias_ref,
    out_ref,
    half_ref,
    rows_of,
    ids_out,
    ids_in,
    serve,
    reply,
    outgoing,
    messages,
    names,
    win_high,
    win_low,
    state,
    send_ids,
    recv_ids,
    send_rows,
    recv_rows,
    send_msgs,
    recv_msgs,
    send_x,
    recv_x,
    send_c,
    recv_c,
):
    node = lax.axis_index("nodes")
    rep = lax.axis_index("rep")
    x, c = rep // 2, rep % 2
    rows, width = memory_ref.shape
    unit = out_ref.shape[1]
    events = cols_ref.shape[0]
    cap = reply.shape[0] // groups
    per = 128 // cap
    tiles = groups // per
    across_x = (node, ((x + 1) % 2) * 2 + c)
    across_c = (node, x * 2 + (c + 1) % 2)

    barrier = pltpu.get_barrier_semaphore()
    partners = [((node + d) % groups, rep) for d in range(1, groups)] + [across_x, across_c]
    for device in partners:
        pl.semaphore_signal(barrier, inc=1, device_id=device, device_id_type=MESH)

    owner = cols_ref[:, 0:1]
    target = cols_ref[:, 1:2]
    source = cols_ref[:, 2:3]
    ticks = cols_ref[:, 3:4]
    lane = lax.broadcasted_iota(jnp.int32, (events, 128), 1).astype(F32)
    row_i = lax.broadcasted_iota(jnp.int32, (events, events), 0)
    col_i = lax.broadcasted_iota(jnp.int32, (events, events), 1)
    named = owner == lane
    before = dot32((row_i > col_i).astype(BF16), named.astype(BF16))
    rank = jnp.sum(jnp.where(named, before, 0.0), axis=1, keepdims=True)
    slot = owner * cap + rank
    place_lane = rank + ((node % per) * cap).astype(F32)
    at_lane = place_lane == lane
    for g in range(groups):
        took = jnp.where(at_lane & (owner == float(g)), target + 1.0, 0.0)
        line = jnp.sum(took, axis=0, keepdims=True) - 1.0
        ids_out[g] = jnp.broadcast_to(line.astype(jnp.int32), (8, 128))
    ids_in[node] = ids_out[node]

    def piece_of(ref, n):
        return ref.at[pl.ds(pl.multiple_of(n * cap, cap), cap), :]

    def send_to(d, src, dst, send, recv):
        return pltpu.make_async_remote_copy(
            src_ref=src,
            dst_ref=dst,
            send_sem=send.at[d - 1],
            recv_sem=recv.at[d - 1],
            device_id=((node + d) % groups, rep),
            device_id_type=MESH,
        )

    def ids_copy(d):
        there = (node + d) % groups
        return send_to(d, ids_out.at[there], ids_in.at[node], send_ids, recv_ids)

    def rows_copy(d):
        there = (node + d) % groups
        return send_to(d, piece_of(serve, there), piece_of(reply, node), send_rows, recv_rows)

    def far_slot():
        return messages.at[rep, pl.ds(pl.multiple_of(events + node * cap, cap), cap), :]

    def msgs_copy(d):
        there = (node + d) % groups
        return send_to(d, piece_of(outgoing, there), far_slot(), send_msgs, recv_msgs)

    def part_of(r, p):
        if p == tiles + 1:
            return names.at[r]
        return messages.at[r, p * 128 : (p + 1) * 128, :]

    def over_x(p):
        return pltpu.make_async_remote_copy(
            src_ref=part_of(rep, p),
            dst_ref=part_of(rep, p),
            send_sem=send_x.at[p],
            recv_sem=recv_x.at[p],
            device_id=across_x,
            device_id_type=MESH,
        )

    def over_c(p, b):
        r = ((x + b) % 2) * 2 + c
        return pltpu.make_async_remote_copy(
            src_ref=part_of(r, p),
            dst_ref=part_of(r, p),
            send_sem=send_c.at[p, b],
            recv_sem=recv_c.at[p, b],
            device_id=across_c,
            device_id_type=MESH,
        )

    started = []

    def start(one):
        one.start()
        started.append(one)

    pl.semaphore_wait(barrier, len(partners))
    for d in range(1, groups):
        start(ids_copy(d))

    rows_of[:, :width] = memory_ref[...].astype(BF16)
    old = jnp.broadcast_to(tick_ref[...], (rows, 128))
    big = jnp.floor(old * (1.0 / 256.0))
    lanes_r = lax.broadcasted_iota(jnp.int32, (rows, 128), 1)
    packed = jnp.where(lanes_r == 0, big, jnp.where(lanes_r == 1, old - big * 256.0, 0.0))
    rows_of[:, width:] = packed.astype(BF16)

    def encoded(found):
        last = found[:, width : width + 1] * 256.0 + found[:, width + 1 : width + 2]
        return jnp.cos((ticks - last) * freq_ref[...] + phase_ref[...]).astype(BF16)

    for d in range(1, groups):
        ids_copy(d).wait_recv()
    row_id = lax.broadcasted_iota(jnp.int32, (rows, 128), 0)
    lines = [src_ref[...]]
    for h in range(tiles):
        line = ids_in[h * per][0:1, :]
        for q in range(1, per):
            line = jnp.maximum(line, ids_in[h * per + q][0:1, :])
        lines.append(line)
        wanted = (row_id == line).astype(BF16)
        serve[h * 128 : (h + 1) * 128, :] = dot_rows(wanted, rows_of[...]).astype(BF16)
    for d in range(1, groups):
        start(rows_copy(d))
    here = pl.ds(pl.multiple_of(node * cap, cap), cap)
    reply[here, :] = serve[here, :]
    blank = jnp.full((8 - len(lines), 128), -1, jnp.int32)
    names[rep] = jnp.concatenate(lines + [blank], axis=0)
    start(over_x(tiles + 1))
    start(over_c(tiles + 1, 0))

    near = (source == lax.broadcasted_iota(jnp.int32, (events, rows), 1).astype(F32)).astype(BF16)
    near = dot32(near, rows_of[...])
    near_rows = near[:, :width].astype(BF16)
    w_first = wm_ref[0:width, :]
    w_second = wm_ref[width : 2 * width, :]
    w_time = wm_ref[2 * width :, :]
    src_sum = dot32(near_rows, w_first) + dot32(encoded(near), w_time)
    dst_sum = dot32(near_rows, w_second)
    chosen = (slot == lax.broadcasted_iota(jnp.int32, (events, groups * cap), 1).astype(F32)).astype(
        BF16
    )

    for d in range(1, groups):
        rows_copy(d).wait_recv()
    far = dot32(chosen, reply[...])
    far_rows = far[:, :width].astype(BF16)
    msg_dst = silu(dst_sum + dot32(far_rows, w_first) + dot32(encoded(far), w_time)).astype(BF16)
    outgoing[...] = dot_rows(chosen, msg_dst).astype(BF16)
    for d in range(1, groups):
        start(msgs_copy(d))
    messages[rep, 0:events, :] = silu(src_sum + dot32(far_rows, w_second)).astype(BF16)
    start(over_x(0))
    start(over_c(0, 0))
    messages[rep, pl.ds(pl.multiple_of(events + node * cap, cap), cap), :] = outgoing[here, :]

    over_x(tiles + 1).wait_recv()
    start(over_c(tiles + 1, 1))
    mem_high, mem_low = split(memory_ref[...])
    for g in range(3):
        place_g = slice(g * unit, (g + 1) * unit)
        high, low = split(wi_ref[g])
        win_high[:, place_g] = high
        win_low[:, place_g] = low
        high, low = split(wh_ref[g])
        state[:, place_g] = dot32(mem_high, high) + dot32(mem_low, high) + dot32(mem_high, low)

    for d in range(1, groups):
        msgs_copy(d).wait_recv()
    for p in range(1, tiles + 1):
        start(over_x(p))
        start(over_c(p, 0))
    for p in range(tiles + 1):
        over_x(p).wait_recv()
        start(over_c(p, 1))
    for p in range(tiles + 2):
        over_c(p, 0).wait_recv()
    for p in range(tiles + 2):
        over_c(p, 1).wait_recv()

    sums = jnp.zeros((rows, messages.shape[2]), F32)
    hits = jnp.zeros((rows, 128), F32)
    for r in range(4):
        tile = names[r]
        parts = [(row_id == tile[p : p + 1, :]).astype(F32) for p in range(tiles + 1)]
        for part in parts:
            hits += part
        sums += dot32(jnp.concatenate(parts, axis=1).astype(BF16), messages[r])
    counts = jnp.sum(hits, axis=1, keepdims=True)
    mean = sums / jnp.maximum(counts, 1.0)
    fed = three_pass(mean, win_high[...], win_low[...])
    was = memory_ref[:, pl.ds(pl.multiple_of(rep * unit, unit), unit)]
    update = sigmoid(fed[:, :unit] + state[:, :unit] + bias_ref[0:1, :])
    reset = sigmoid(fed[:, unit : 2 * unit] + state[:, unit : 2 * unit] + bias_ref[1:2, :])
    cand = jnp.tanh(
        fed[:, 2 * unit :] + bias_ref[2:3, :] + reset * (state[:, 2 * unit :] + bias_ref[3:4, :])
    )
    fresh = (1.0 - update) * cand + update * was
    fresh = jnp.where(counts > 0.0, fresh, was)
    out_ref[...] = fresh
    half_ref[...] = fresh.astype(BF16)
    for one in started:
        one.wait_send()


def update_rows(memory, tick, cols, src, freq, phase, wm, wi, wh, bias, groups):
    rows, width = memory.shape
    unit = bias.shape[1]
    events = cols.shape[0]
    cap = 2 * events // groups
    slots = groups * cap
    pieces = events // 128 + slots // 128
    msg = wm.shape[1]
    dma = pltpu.SemaphoreType.DMA
    counts = [(groups - 1,)] * 3 + [(pieces + 1,), (pieces + 1, 2)]
    return pl.pallas_call(
        functools.partial(update_kernel, groups),
        out_shape=(
            jax.ShapeDtypeStruct((rows, unit), F32),
            jax.ShapeDtypeStruct((rows, unit), BF16),
        ),
        in_specs=[pl.BlockSpec(memory_space=pltpu.VMEM)] * 10,
        out_specs=(pl.BlockSpec(memory_space=pltpu.VMEM),) * 2,
        scratch_shapes=[
            pltpu.VMEM((rows, width + 128), BF16),
            pltpu.VMEM((groups, 8, 128), jnp.int32),
            pltpu.VMEM((groups, 8, 128), jnp.int32),
            pltpu.VMEM((slots, width + 128), BF16),
            pltpu.VMEM((slots, width + 128), BF16),
            pltpu.VMEM((slots, msg), BF16),
            pltpu.VMEM((4, events + slots, msg), BF16),
            pltpu.VMEM((4, 8, 128), jnp.int32),
            pltpu.VMEM((msg, 3 * unit), BF16),
            pltpu.VMEM((msg, 3 * unit), BF16),
            pltpu.VMEM((rows, 3 * unit), F32),
        ]
        + [dma(shape) for shape in counts for _ in range(2)],
        compiler_params=pltpu.CompilerParams(
            collective_id=0, has_side_effects=True, vmem_limit_bytes=40 * 1024 * 1024
        ),
    )(memory, tick, cols, src, freq, phase, wm, wi, wh, bias)


def encode(gaps, freq, phase):
    return jnp.cos(gaps[..., None] * freq + phase)


def place(owner, groups, capacity):
    onehot = (owner[:, None] == jnp.arange(groups, dtype=jnp.int32)[None, :]).astype(jnp.int32)
    before = jnp.cumsum(onehot, axis=0) - onehot
    return owner * capacity + jnp.sum(before * onehot, axis=1)


def message_pair(src_rows, dst_rows, src_time, dst_time, w_message):
    count = src_rows.shape[0]
    stacked = jnp.concatenate(
        [
            jnp.concatenate([src_rows, dst_rows, src_time], axis=1),
            jnp.concatenate([dst_rows, src_rows, dst_time], axis=1),
        ],
        axis=0,
    )
    messages = jax.nn.silu(jnp.dot(stacked, w_message, preferred_element_type=jnp.float32)).astype(
        jnp.bfloat16
    )
    return (messages[:count], messages[count:])


def on_device_large(
    memory,
    last_tick,
    src_local,
    dst_owner,
    dst_local,
    event_tick,
    nbr_owner,
    nbr_local,
    nbr_tick,
    freq,
    phase,
    w_message,
    gru_input,
    gru_hidden,
    gru_bias,
    w_query,
    w_keyval_mem,
    w_keyval_time,
):
    groups = lax.axis_size("nodes")
    events = src_local.shape[0]
    rows_here = memory.shape[0]
    width_m = memory.shape[1]
    neighbours = nbr_local.shape[1]
    msg_width = w_message.shape[1]
    dst_cap = max(2, 2 * events // groups)
    nbr_cap = 2 * events * neighbours // groups
    dst_slot = place(dst_owner[:, 0], groups, dst_cap)
    nbr_slot = place(nbr_owner.reshape(-1), groups, nbr_cap)
    dst_ids = (
        jnp.full((groups * dst_cap,), -1, jnp.int32)
        .at[dst_slot]
        .set(dst_local)
        .reshape(groups, dst_cap)
    )
    nbr_ids = (
        jnp.full((groups * nbr_cap,), -1, jnp.int32)
        .at[nbr_slot]
        .set(nbr_local.reshape(-1))
        .reshape(groups, nbr_cap)
    )
    mem_half = memory.astype(jnp.bfloat16)
    near_rows = mem_half[src_local]
    near_ticks = last_tick[src_local]
    ticks = event_tick.astype(jnp.float32)
    got_dst, got_nbr = (
        lax.all_to_all(dst_ids, "nodes", split_axis=0, concat_axis=0, tiled=True),
        lax.all_to_all(nbr_ids, "nodes", split_axis=0, concat_axis=0, tiled=True),
    )
    safe_dst = jnp.maximum(got_dst, 0)
    reply_rows, reply_ticks = (
        lax.all_to_all(mem_half[safe_dst], "nodes", split_axis=0, concat_axis=0, tiled=True),
        lax.all_to_all(last_tick[safe_dst], "nodes", split_axis=0, concat_axis=0, tiled=True),
    )
    far_rows = reply_rows.reshape(-1, width_m)[dst_slot]
    far_ticks = reply_ticks.reshape(-1)[dst_slot]
    src_time = encode(ticks - near_ticks.astype(jnp.float32), freq, phase).astype(jnp.bfloat16)
    dst_time = encode(ticks - far_ticks.astype(jnp.float32), freq, phase).astype(jnp.bfloat16)
    msg_src, msg_dst = message_pair(near_rows, far_rows, src_time, dst_time, w_message)
    outgoing = (
        jnp.zeros((groups * dst_cap, msg_width), jnp.bfloat16)
        .at[dst_slot]
        .set(msg_dst)
        .reshape(groups, dst_cap, msg_width)
    )
    incoming = lax.all_to_all(outgoing, "nodes", split_axis=0, concat_axis=0, tiled=True)
    far_msgs = incoming.reshape(-1, msg_width)
    row_ids = jnp.arange(rows_here, dtype=jnp.int32)[:, None]
    hit_far = (row_ids == got_dst.reshape(1, -1)).astype(jnp.bfloat16)
    hit_near = (row_ids == src_local[None, :]).astype(jnp.bfloat16)
    sums = jnp.dot(hit_near, msg_src, preferred_element_type=jnp.float32) + jnp.dot(
        hit_far, far_msgs, preferred_element_type=jnp.float32
    )
    counts = jnp.sum(hit_near.astype(jnp.float32), axis=1) + jnp.sum(
        hit_far.astype(jnp.float32), axis=1
    )
    sums, counts = lax.psum((sums, counts), "rep")
    unit_width = gru_bias.shape[1]
    start = lax.axis_index("rep") * unit_width
    state_part = lax.dynamic_slice_in_dim(memory, start, unit_width, 1)
    mean = sums / jnp.maximum(counts, 1.0)[:, None]
    highest = lax.Precision.HIGHEST
    a_parts = jnp.einsum("rk,gku->gru", mean, gru_input, precision=highest)
    b_parts = jnp.einsum("rk,gku->gru", memory, gru_hidden, precision=highest)
    update = jax.nn.sigmoid(a_parts[0] + b_parts[0] + gru_bias[0])
    reset = jax.nn.sigmoid(a_parts[1] + b_parts[1] + gru_bias[1])
    cand = jnp.tanh(a_parts[2] + gru_bias[2] + reset * (b_parts[2] + gru_bias[3]))
    fresh = (1.0 - update) * cand + update * state_part
    new_part = jnp.where((counts > 0.0)[:, None], fresh, state_part)
    updated = lax.all_gather(new_part.astype(jnp.bfloat16), "rep", axis=1, tiled=True)
    served = updated[jnp.maximum(got_nbr, 0)]
    returned = lax.all_to_all(served, "nodes", split_axis=0, concat_axis=0, tiled=True)
    fetched = returned.reshape(-1, updated.shape[1])[nbr_slot]
    kv_mem = jnp.dot(fetched, w_keyval_mem, preferred_element_type=jnp.float32).astype(jnp.bfloat16)
    kv_mem = lax.optimization_barrier(kv_mem).astype(jnp.float32)
    gaps = ticks[:, None] - nbr_tick.astype(jnp.float32)
    time_enc = encode(gaps, freq, phase).reshape(-1, freq.shape[0]).astype(jnp.bfloat16)
    kv_time = jnp.dot(time_enc, w_keyval_time, preferred_element_type=jnp.float32)
    keyval = (kv_mem + kv_time).reshape(events, neighbours, 2, HEADS, HEAD_DIM)
    query = jnp.dot(updated[src_local], w_query, preferred_element_type=jnp.float32).astype(
        jnp.bfloat16
    )
    query = lax.optimization_barrier(query).astype(jnp.float32).reshape(events, HEADS, HEAD_DIM)
    scores = jnp.einsum("ehd,ejhd->ehj", query, keyval[:, :, 0]) / math.sqrt(HEAD_DIM)
    weights = jax.nn.softmax(scores, axis=-1)
    mixed = jnp.einsum("ehj,ejhd->ehd", weights, keyval[:, :, 1])
    embed = mixed.reshape(events, HEADS * HEAD_DIM).astype(jnp.bfloat16)
    return (new_part, embed)


def on_device(
    memory,
    last_tick,
    src_local,
    dst_owner,
    dst_local,
    event_tick,
    nbr_owner,
    nbr_local,
    nbr_tick,
    freq,
    phase,
    w_message,
    gru_input,
    gru_hidden,
    gru_bias,
    w_query,
    w_keyval_mem,
    w_keyval_time,
):
    groups = lax.axis_size("nodes")
    rows_here = memory.shape[0]
    ticks = event_tick.astype(jnp.float32)
    cols = jnp.stack(
        [dst_owner[:, 0].astype(F32), dst_local.astype(F32), src_local.astype(F32), ticks], axis=1
    )
    new_part, new_half = update_rows(
        memory,
        last_tick.astype(F32)[:, None],
        cols,
        src_local[None, :],
        freq[None, :],
        phase[None, :],
        w_message,
        gru_input,
        gru_hidden,
        gru_bias,
        groups,
    )
    index = (nbr_owner[:, :, 0] * rows_here + nbr_local).astype(jnp.float32)
    gaps = ticks[:, None] - nbr_tick.astype(jnp.float32)
    embed = attend(
        new_half,
        src_local[:, None],
        index,
        gaps,
        freq[None, :],
        phase[None, :],
        w_query,
        w_keyval_mem,
        w_keyval_time,
        groups,
        lax.axis_size("rep"),
    )
    return (new_part, embed)


def solution(mesh):
    placed = (
        P("nodes", None),
        P("nodes"),
        P(("nodes", "rep")),
        P(("nodes", "rep"), None),
        P(("nodes", "rep")),
        P(("nodes", "rep")),
        P(("nodes", "rep"), None, None),
        P(("nodes", "rep"), None),
        P(("nodes", "rep"), None),
        P(),
        P(),
        P(),
        P(None, None, "rep"),
        P(None, None, "rep"),
        P(None, "rep"),
        P(),
        P(),
        P(),
    )
    fits = mesh.shape["nodes"] == 8 and mesh.shape["rep"] == 4
    return jax.shard_map(
        on_device if fits else on_device_large,
        mesh=mesh,
        in_specs=placed,
        out_specs=(P("nodes", "rep"), P(("nodes", "rep"), None)),
        check_vma=False,
    )
```

```python
import functools
import math

import jax
import jax.numpy as jnp
from jax import lax
from jax.experimental import pallas as pl
from jax.experimental.pallas import tpu as pltpu
from jax.sharding import PartitionSpec as P

HEADS = 8
HEAD_DIM = 64
MESH = pl.DeviceIdType.MESH
F32 = jnp.float32
BF16 = jnp.bfloat16


def dot32(a, b):
    return jnp.dot(a, b, preferred_element_type=F32)


def split(v):
    high = v.astype(BF16)
    return high, (v - high.astype(F32)).astype(BF16)


def column(ref, j, count):
    lanes = lax.broadcasted_iota(jnp.int32, ref.shape, 1)
    value = ref[...]
    cols = [
        jnp.sum(jnp.where(lanes == j + i, value, 0.0), axis=1, keepdims=True) for i in range(count)
    ]
    return jnp.concatenate(cols, axis=0)


def attend_kernel(
    groups,
    part_ref,
    src_ref,
    index_ref,
    gap_ref,
    freq_ref,
    phase_ref,
    wq_hbm,
    wkv_hbm,
    wt_hbm,
    out_ref,
    wq_ref,
    wkv_ref,
    wt_ref,
    load_sem,
    table,
    found,
    keyval,
    scores,
    send_z,
    recv_z,
    send_a,
    recv_a,
    send_b,
    recv_b,
    send_c,
    recv_c,
):
    pairs = [(wt_hbm, wt_ref), (wq_hbm, wq_ref), (wkv_hbm, wkv_ref)]
    loads = [pltpu.make_async_copy(a, b, load_sem.at[i]) for i, (a, b) in enumerate(pairs)]
    for load in loads:
        load.start()
    node = lax.axis_index("nodes")
    rep = lax.axis_index("rep")
    deep = groups // 2
    z, y = node // 2, node % 2
    x, c = rep // 2, rep % 2
    rows, unit = part_ref.shape
    half = rows // 2
    events, neighbours = index_ref.shape
    width = table.shape[1]

    def where_of(h, d, k, b):
        zz = (z + deep - d) % deep
        ky, kx = (k, b) if h == 0 else (b, k)
        return zz * 2 + (y + ky) % 2, (x + kx) % 2

    def block(n, r, h):
        return table.at[
            pl.ds(pl.multiple_of(n * rows + h * half, half), half),
            pl.ds(pl.multiple_of(r * unit, unit), unit),
        ]

    def copy(n, r, h, device, send, recv):
        return pltpu.make_async_remote_copy(
            src_ref=block(n, r, h),
            dst_ref=block(n, r, h),
            send_sem=send,
            recv_sem=recv,
            device_id=device,
            device_id_type=MESH,
        )

    across_y = (z * 2 + (y + 1) % 2, rep)
    across_x = (node, ((x + 1) % 2) * 2 + c)
    across_c = (node, x * 2 + (c + 1) % 2)

    def along_z(h, d):
        device = (((z + d) % deep) * 2 + y, rep)
        return copy(node, rep, h, device, send_z.at[h, d], recv_z.at[h, d])

    def first(h, d):
        n, xx = where_of(h, d, 0, 0)
        device = across_y if h == 0 else across_x
        return copy(n, xx * 2 + c, h, device, send_a.at[h, d], recv_a.at[h, d])

    def second(h, d, k):
        n, xx = where_of(h, d, k, 0)
        device = across_x if h == 0 else across_y
        return copy(n, xx * 2 + c, h, device, send_b.at[h, d, k], recv_b.at[h, d, k])

    def core(h, d, k, b):
        n, xx = where_of(h, d, k, b)
        i = k * 2 + b
        return copy(n, xx * 2 + c, h, across_c, send_c.at[h, d, i], recv_c.at[h, d, i])

    block_rows = pl.ds(pl.multiple_of(node * rows, rows), rows)
    table[block_rows, pl.ds(pl.multiple_of(rep * unit, unit), unit)] = part_ref[...]

    partners = [(((z + d) % deep) * 2 + y, rep) for d in range(1, deep)]
    partners += [across_y, across_x, across_c]
    barrier = pltpu.get_barrier_semaphore()
    for device in partners:
        pl.semaphore_signal(barrier, inc=1, device_id=device, device_id_type=MESH)
    pl.semaphore_wait(barrier, len(partners))

    started = []

    def start(one):
        one.start()
        started.append(one)

    batch = 4

    def time_part(g):
        gaps = column(gap_ref, g * batch, batch)
        enc = jnp.cos(gaps * freq_ref[...] + phase_ref[...]).astype(BF16)
        size = batch * events
        keyval[g * size : (g + 1) * size, :] = dot32(enc, wt_ref[...])

    steps = neighbours // batch
    for d in range(1, deep):
        for h in range(2):
            start(along_z(h, d))
    for h in range(2):
        start(first(h, 0))
        start(second(h, 0, 0))
        start(core(h, 0, 0, 0))
    for load in loads:
        load.wait()
    time_part(0)
    for d in range(1, deep):
        for h in range(2):
            along_z(h, d).wait_recv()
            start(first(h, d))
            start(second(h, d, 0))
            start(core(h, d, 0, 0))
        if d < steps:
            time_part(d)
    for g in range(deep, steps):
        time_part(g)

    size = batch * events
    lanes = lax.broadcasted_iota(jnp.int32, (size, rows), 1)

    def forward_first(d):
        for h in range(2):
            first(h, d).wait_recv()
            start(second(h, d, 1))
            start(core(h, d, 1, 0))

    def forward_second(d):
        for k in range(2):
            for h in range(2):
                second(h, d, k).wait_recv()
                start(core(h, d, k, 1))

    def look_up(d):
        for k in range(2):
            for b in range(2):
                for h in range(2):
                    core(h, d, k, b).wait_recv()

        @pl.loop(0, steps)
        def _(g):
            names = column(index_ref, g * batch, batch).astype(jnp.int32)
            here = pl.ds(pl.multiple_of(g * size, size), size)
            total = jnp.zeros((size, width), F32)
            for k in range(2):
                n, _ = where_of(0, d, k, 0)
                chosen = (names - n * rows == lanes).astype(BF16)
                total += dot32(chosen, table[pl.ds(pl.multiple_of(n * rows, rows), rows), :])
            if d > 0:
                total += found[here, :].astype(F32)
            found[here, :] = total.astype(BF16)

    forward_first(0)
    forward_second(0)
    for d in range(1, deep):
        forward_first(d)
        look_up(d - 1)
        forward_second(d)
    lane_row = lax.broadcasted_iota(jnp.int32, (events, rows), 1)
    hit = (src_ref[...] == lane_row).astype(BF16)
    mine = dot32(hit, table[block_rows, :]).astype(BF16)
    query = dot32(mine, wq_ref[...]).astype(BF16).astype(F32) * (1.0 / math.sqrt(HEAD_DIM))
    query = jnp.concatenate([query] * batch, axis=0)
    look_up(deep - 1)
    for one in started:
        one.wait_send()

    att = HEADS * HEAD_DIM
    head_sum = (
        lax.broadcasted_iota(jnp.int32, (att, 128), 0) // HEAD_DIM
        == lax.broadcasted_iota(jnp.int32, (att, 128), 1)
    ).astype(BF16)
    head_spread = (
        lax.broadcasted_iota(jnp.int32, (128, att), 1) // HEAD_DIM
        == lax.broadcasted_iota(jnp.int32, (128, att), 0)
    ).astype(BF16)

    @pl.loop(0, steps)
    def _(g):
        here = pl.ds(pl.multiple_of(g * size, size), size)
        kv = dot32(found[here, :], wkv_ref[...]).astype(BF16).astype(F32)
        kv = kv + keyval[here, :]
        keyval[here, att:] = kv[:, att:]
        high, low = split(query * kv[:, :att])
        scores[here, :] = dot32(high, head_sum) + dot32(low, head_sum)

    top = scores[0:events, :]
    for j in range(1, neighbours):
        top = jnp.maximum(top, scores[j * events : (j + 1) * events, :])
    total = jnp.zeros_like(top)
    for j in range(neighbours):
        term = jnp.exp(scores[j * events : (j + 1) * events, :] - top)
        scores[j * events : (j + 1) * events, :] = term
        total += term
    mixed = jnp.zeros((events, att), F32)
    for g in range(steps):
        high, low = split(scores[g * size : (g + 1) * size, :])
        spread = dot32(high, head_spread) + dot32(low, head_spread)
        terms = spread * keyval[g * size : (g + 1) * size, att:]
        for i in range(batch):
            mixed += terms[i * events : (i + 1) * events, :]
    high, low = split(1.0 / total)
    scale = dot32(high, head_spread) + dot32(low, head_spread)
    out_ref[...] = (mixed * scale).astype(out_ref.dtype)


def attend(part, src, index, gaps, freq, phase, wq, wkv, wt, groups, reps):
    rows, unit = part.shape
    events, neighbours = index.shape
    deep = groups // 2
    total = groups * rows
    dma = pltpu.SemaphoreType.DMA
    pairs = [(2, deep), (2, deep), (2, deep, 2), (2, deep, 4)]
    sems = [dma(shape) for shape in pairs for _ in range(2)]
    return pl.pallas_call(
        functools.partial(attend_kernel, groups),
        out_shape=jax.ShapeDtypeStruct((events, HEADS * HEAD_DIM), BF16),
        in_specs=[
            pl.BlockSpec(memory_space=pltpu.HBM if i > 5 else pltpu.VMEM) for i in range(9)
        ],
        out_specs=pl.BlockSpec(memory_space=pltpu.VMEM),
        scratch_shapes=[pltpu.VMEM(v.shape, v.dtype) for v in (wq, wkv, wt)]
        + [
            dma((3,)),
            pltpu.VMEM((total, reps * unit), BF16),
            pltpu.VMEM((events * neighbours, reps * unit), BF16),
            pltpu.VMEM((events * neighbours, wkv.shape[1]), F32),
            pltpu.VMEM((events * neighbours, 128), F32),
        ]
        + sems,
        compiler_params=pltpu.CompilerParams(
            collective_id=1, has_side_effects=True, vmem_limit_bytes=62 * 1024 * 1024
        ),
    )(part, src, index, gaps, freq, phase, wq, wkv, wt)


def dot_rows(a, b):
    return lax.dot_general(a, b, (((0,), (0,)), ((), ())), preferred_element_type=F32)


def three_pass(a, b_high, b_low):
    high, low = split(a)
    return dot32(high, b_high) + dot32(low, b_high) + dot32(high, b_low)


def silu(v):
    return v / (1.0 + jnp.exp(-v))


def sigmoid(v):
    return 1.0 / (1.0 + jnp.exp(-v))


def update_kernel(
    groups,
    memory_hbm,
    tick_ref,
    cols_ref,
    src_ref,
    freq_ref,
    phase_ref,
    wm_hbm,
    wi_hbm,
    wh_hbm,
    bias_ref,
    out_ref,
    half_ref,
    memory_ref,
    wm_ref,
    wi_ref,
    wh_ref,
    load_sem,
    rows_of,
    ids_out,
    ids_in,
    serve,
    reply,
    outgoing,
    messages,
    names,
    win_high,
    win_low,
    state,
    send_ids,
    recv_ids,
    send_rows,
    recv_rows,
    send_msgs,
    recv_msgs,
    send_x,
    recv_x,
    send_c,
    recv_c,
):
    node = lax.axis_index("nodes")
    rep = lax.axis_index("rep")
    x, c = rep // 2, rep % 2
    rows, width = memory_ref.shape
    unit = out_ref.shape[1]
    events = cols_ref.shape[0]
    cap = reply.shape[0] // groups
    per = 128 // cap
    tiles = groups // per
    across_x = (node, ((x + 1) % 2) * 2 + c)
    across_c = (node, x * 2 + (c + 1) % 2)

    pairs = [(memory_hbm, memory_ref), (wm_hbm, wm_ref), (wh_hbm, wh_ref), (wi_hbm, wi_ref)]
    loads = [pltpu.make_async_copy(a, b, load_sem.at[i]) for i, (a, b) in enumerate(pairs)]
    for load in loads:
        load.start()

    barrier = pltpu.get_barrier_semaphore()
    partners = [((node + d) % groups, rep) for d in range(1, groups)] + [across_x, across_c]
    for device in partners:
        pl.semaphore_signal(barrier, inc=1, device_id=device, device_id_type=MESH)

    owner = cols_ref[:, 0:1]
    target = cols_ref[:, 1:2]
    source = cols_ref[:, 2:3]
    ticks = cols_ref[:, 3:4]
    lane = lax.broadcasted_iota(jnp.int32, (events, 128), 1).astype(F32)
    row_i = lax.broadcasted_iota(jnp.int32, (events, events), 0)
    col_i = lax.broadcasted_iota(jnp.int32, (events, events), 1)
    named = owner == lane
    before = dot32((row_i > col_i).astype(BF16), named.astype(BF16))
    rank = jnp.sum(jnp.where(named, before, 0.0), axis=1, keepdims=True)
    slot = owner * cap + rank
    place_lane = rank + ((node % per) * cap).astype(F32)
    at_lane = place_lane == lane
    for g in range(groups):
        took = jnp.where(at_lane & (owner == float(g)), target + 1.0, 0.0)
        line = jnp.sum(took, axis=0, keepdims=True) - 1.0
        ids_out[g] = jnp.broadcast_to(line.astype(jnp.int32), (8, 128))
    ids_in[node] = ids_out[node]

    def piece_of(ref, n):
        return ref.at[pl.ds(pl.multiple_of(n * cap, cap), cap), :]

    def send_to(d, src, dst, send, recv):
        return pltpu.make_async_remote_copy(
            src_ref=src,
            dst_ref=dst,
            send_sem=send.at[d - 1],
            recv_sem=recv.at[d - 1],
            device_id=((node + d) % groups, rep),
            device_id_type=MESH,
        )

    def ids_copy(d):
        there = (node + d) % groups
        return send_to(d, ids_out.at[there], ids_in.at[node], send_ids, recv_ids)

    def rows_copy(d):
        there = (node + d) % groups
        return send_to(d, piece_of(serve, there), piece_of(reply, node), send_rows, recv_rows)

    def far_slot():
        return messages.at[rep, pl.ds(pl.multiple_of(events + node * cap, cap), cap), :]

    def msgs_copy(d):
        there = (node + d) % groups
        return send_to(d, piece_of(outgoing, there), far_slot(), send_msgs, recv_msgs)

    def part_of(r, p):
        if p == tiles + 1:
            return names.at[r]
        return messages.at[r, p * 128 : (p + 1) * 128, :]

    def over_x(p):
        return pltpu.make_async_remote_copy(
            src_ref=part_of(rep, p),
            dst_ref=part_of(rep, p),
            send_sem=send_x.at[p],
            recv_sem=recv_x.at[p],
            device_id=across_x,
            device_id_type=MESH,
        )

    def over_c(p, b):
        r = ((x + b) % 2) * 2 + c
        return pltpu.make_async_remote_copy(
            src_ref=part_of(r, p),
            dst_ref=part_of(r, p),
            send_sem=send_c.at[p, b],
            recv_sem=recv_c.at[p, b],
            device_id=across_c,
            device_id_type=MESH,
        )

    started = []

    def start(one):
        one.start()
        started.append(one)

    pl.semaphore_wait(barrier, len(partners))
    for d in range(1, groups):
        start(ids_copy(d))

    loads[0].wait()
    rows_of[:, :width] = memory_ref[...].astype(BF16)
    old = jnp.broadcast_to(tick_ref[...], (rows, 128))
    big = jnp.floor(old * (1.0 / 256.0))
    lanes_r = lax.broadcasted_iota(jnp.int32, (rows, 128), 1)
    packed = jnp.where(lanes_r == 0, big, jnp.where(lanes_r == 1, old - big * 256.0, 0.0))
    rows_of[:, width:] = packed.astype(BF16)

    def encoded(found):
        last = found[:, width : width + 1] * 256.0 + found[:, width + 1 : width + 2]
        return jnp.cos((ticks - last) * freq_ref[...] + phase_ref[...]).astype(BF16)

    for d in range(1, groups):
        ids_copy(d).wait_recv()
    row_id = lax.broadcasted_iota(jnp.int32, (rows, 128), 0)
    lines = [src_ref[...]]
    for h in range(tiles):
        line = ids_in[h * per][0:1, :]
        for q in range(1, per):
            line = jnp.maximum(line, ids_in[h * per + q][0:1, :])
        lines.append(line)
        wanted = (row_id == line).astype(BF16)
        serve[h * 128 : (h + 1) * 128, :] = dot_rows(wanted, rows_of[...]).astype(BF16)
    for d in range(1, groups):
        start(rows_copy(d))
    here = pl.ds(pl.multiple_of(node * cap, cap), cap)
    reply[here, :] = serve[here, :]
    blank = jnp.full((8 - len(lines), 128), -1, jnp.int32)
    names[rep] = jnp.concatenate(lines + [blank], axis=0)
    start(over_x(tiles + 1))
    start(over_c(tiles + 1, 0))

    near = (source == lax.broadcasted_iota(jnp.int32, (events, rows), 1).astype(F32)).astype(BF16)
    near = dot32(near, rows_of[...])
    near_rows = near[:, :width].astype(BF16)
    loads[1].wait()
    w_first = wm_ref[0:width, :]
    w_second = wm_ref[width : 2 * width, :]
    w_time = wm_ref[2 * width :, :]
    src_sum = dot32(near_rows, w_first) + dot32(encoded(near), w_time)
    dst_sum = dot32(near_rows, w_second)
    chosen = (slot == lax.broadcasted_iota(jnp.int32, (events, groups * cap), 1).astype(F32)).astype(
        BF16
    )

    for d in range(1, groups):
        rows_copy(d).wait_recv()
    far = dot32(chosen, reply[...])
    far_rows = far[:, :width].astype(BF16)
    msg_dst = silu(dst_sum + dot32(far_rows, w_first) + dot32(encoded(far), w_time)).astype(BF16)
    outgoing[...] = dot_rows(chosen, msg_dst).astype(BF16)
    for d in range(1, groups):
        start(msgs_copy(d))
    messages[rep, 0:events, :] = silu(src_sum + dot32(far_rows, w_second)).astype(BF16)
    start(over_x(0))
    start(over_c(0, 0))
    messages[rep, pl.ds(pl.multiple_of(events + node * cap, cap), cap), :] = outgoing[here, :]

    over_x(tiles + 1).wait_recv()
    start(over_c(tiles + 1, 1))
    loads[2].wait()
    loads[3].wait()
    mem_high, mem_low = split(memory_ref[...])
    for g in range(3):
        place_g = slice(g * unit, (g + 1) * unit)
        high, low = split(wi_ref[g])
        win_high[:, place_g] = high
        win_low[:, place_g] = low
        high, low = split(wh_ref[g])
        state[:, place_g] = dot32(mem_high, high) + dot32(mem_low, high) + dot32(mem_high, low)

    for d in range(1, groups):
        msgs_copy(d).wait_recv()
    for p in range(1, tiles + 1):
        start(over_x(p))
        start(over_c(p, 0))
    for p in range(tiles + 1):
        over_x(p).wait_recv()
        start(over_c(p, 1))
    for p in range(tiles + 2):
        over_c(p, 0).wait_recv()
    for p in range(tiles + 2):
        over_c(p, 1).wait_recv()

    sums = jnp.zeros((rows, messages.shape[2]), F32)
    hits = jnp.zeros((rows, 128), F32)
    for r in range(4):
        tile = names[r]
        parts = [(row_id == tile[p : p + 1, :]).astype(F32) for p in range(tiles + 1)]
        for part in parts:
            hits += part
        sums += dot32(jnp.concatenate(parts, axis=1).astype(BF16), messages[r])
    counts = jnp.sum(hits, axis=1, keepdims=True)
    mean = sums / jnp.maximum(counts, 1.0)
    fed = three_pass(mean, win_high[...], win_low[...])
    was = memory_ref[:, pl.ds(pl.multiple_of(rep * unit, unit), unit)]
    update = sigmoid(fed[:, :unit] + state[:, :unit] + bias_ref[0:1, :])
    reset = sigmoid(fed[:, unit : 2 * unit] + state[:, unit : 2 * unit] + bias_ref[1:2, :])
    cand = jnp.tanh(
        fed[:, 2 * unit :] + bias_ref[2:3, :] + reset * (state[:, 2 * unit :] + bias_ref[3:4, :])
    )
    fresh = (1.0 - update) * cand + update * was
    fresh = jnp.where(counts > 0.0, fresh, was)
    out_ref[...] = fresh
    half_ref[...] = fresh.astype(BF16)
    for one in started:
        one.wait_send()


def update_rows(memory, tick, cols, src, freq, phase, wm, wi, wh, bias, groups):
    rows, width = memory.shape
    unit = bias.shape[1]
    events = cols.shape[0]
    cap = 2 * events // groups
    slots = groups * cap
    pieces = events // 128 + slots // 128
    msg = wm.shape[1]
    dma = pltpu.SemaphoreType.DMA
    counts = [(groups - 1,)] * 3 + [(pieces + 1,), (pieces + 1, 2)]
    return pl.pallas_call(
        functools.partial(update_kernel, groups),
        out_shape=(
            jax.ShapeDtypeStruct((rows, unit), F32),
            jax.ShapeDtypeStruct((rows, unit), BF16),
        ),
        in_specs=[
            pl.BlockSpec(memory_space=pltpu.HBM if i in (0, 6, 7, 8) else pltpu.VMEM)
            for i in range(10)
        ],
        out_specs=(pl.BlockSpec(memory_space=pltpu.VMEM),) * 2,
        scratch_shapes=[pltpu.VMEM(v.shape, v.dtype) for v in (memory, wm, wi, wh)]
        + [
            dma((4,)),
            pltpu.VMEM((rows, width + 128), BF16),
            pltpu.VMEM((groups, 8, 128), jnp.int32),
            pltpu.VMEM((groups, 8, 128), jnp.int32),
            pltpu.VMEM((slots, width + 128), BF16),
            pltpu.VMEM((slots, width + 128), BF16),
            pltpu.VMEM((slots, msg), BF16),
            pltpu.VMEM((4, events + slots, msg), BF16),
            pltpu.VMEM((4, 8, 128), jnp.int32),
            pltpu.VMEM((msg, 3 * unit), BF16),
            pltpu.VMEM((msg, 3 * unit), BF16),
            pltpu.VMEM((rows, 3 * unit), F32),
        ]
        + [dma(shape) for shape in counts for _ in range(2)],
        compiler_params=pltpu.CompilerParams(
            collective_id=0, has_side_effects=True, vmem_limit_bytes=62 * 1024 * 1024
        ),
    )(memory, tick, cols, src, freq, phase, wm, wi, wh, bias)


def encode(gaps, freq, phase):
    return jnp.cos(gaps[..., None] * freq + phase)


def place(owner, groups, capacity):
    onehot = (owner[:, None] == jnp.arange(groups, dtype=jnp.int32)[None, :]).astype(jnp.int32)
    before = jnp.cumsum(onehot, axis=0) - onehot
    return owner * capacity + jnp.sum(before * onehot, axis=1)


def message_pair(src_rows, dst_rows, src_time, dst_time, w_message):
    count = src_rows.shape[0]
    stacked = jnp.concatenate(
        [
            jnp.concatenate([src_rows, dst_rows, src_time], axis=1),
            jnp.concatenate([dst_rows, src_rows, dst_time], axis=1),
        ],
        axis=0,
    )
    messages = jax.nn.silu(jnp.dot(stacked, w_message, preferred_element_type=jnp.float32)).astype(
        jnp.bfloat16
    )
    return (messages[:count], messages[count:])


def on_device_large(
    memory,
    last_tick,
    src_local,
    dst_owner,
    dst_local,
    event_tick,
    nbr_owner,
    nbr_local,
    nbr_tick,
    freq,
    phase,
    w_message,
    gru_input,
    gru_hidden,
    gru_bias,
    w_query,
    w_keyval_mem,
    w_keyval_time,
):
    groups = lax.axis_size("nodes")
    events = src_local.shape[0]
    rows_here = memory.shape[0]
    width_m = memory.shape[1]
    neighbours = nbr_local.shape[1]
    msg_width = w_message.shape[1]
    dst_cap = max(2, 2 * events // groups)
    nbr_cap = 2 * events * neighbours // groups
    dst_slot = place(dst_owner[:, 0], groups, dst_cap)
    nbr_slot = place(nbr_owner.reshape(-1), groups, nbr_cap)
    dst_ids = (
        jnp.full((groups * dst_cap,), -1, jnp.int32)
        .at[dst_slot]
        .set(dst_local)
        .reshape(groups, dst_cap)
    )
    nbr_ids = (
        jnp.full((groups * nbr_cap,), -1, jnp.int32)
        .at[nbr_slot]
        .set(nbr_local.reshape(-1))
        .reshape(groups, nbr_cap)
    )
    mem_half = memory.astype(jnp.bfloat16)
    near_rows = mem_half[src_local]
    near_ticks = last_tick[src_local]
    ticks = event_tick.astype(jnp.float32)
    got_dst, got_nbr = (
        lax.all_to_all(dst_ids, "nodes", split_axis=0, concat_axis=0, tiled=True),
        lax.all_to_all(nbr_ids, "nodes", split_axis=0, concat_axis=0, tiled=True),
    )
    safe_dst = jnp.maximum(got_dst, 0)
    reply_rows, reply_ticks = (
        lax.all_to_all(mem_half[safe_dst], "nodes", split_axis=0, concat_axis=0, tiled=True),
        lax.all_to_all(last_tick[safe_dst], "nodes", split_axis=0, concat_axis=0, tiled=True),
    )
    far_rows = reply_rows.reshape(-1, width_m)[dst_slot]
    far_ticks = reply_ticks.reshape(-1)[dst_slot]
    src_time = encode(ticks - near_ticks.astype(jnp.float32), freq, phase).astype(jnp.bfloat16)
    dst_time = encode(ticks - far_ticks.astype(jnp.float32), freq, phase).astype(jnp.bfloat16)
    msg_src, msg_dst = message_pair(near_rows, far_rows, src_time, dst_time, w_message)
    outgoing = (
        jnp.zeros((groups * dst_cap, msg_width), jnp.bfloat16)
        .at[dst_slot]
        .set(msg_dst)
        .reshape(groups, dst_cap, msg_width)
    )
    incoming = lax.all_to_all(outgoing, "nodes", split_axis=0, concat_axis=0, tiled=True)
    far_msgs = incoming.reshape(-1, msg_width)
    row_ids = jnp.arange(rows_here, dtype=jnp.int32)[:, None]
    hit_far = (row_ids == got_dst.reshape(1, -1)).astype(jnp.bfloat16)
    hit_near = (row_ids == src_local[None, :]).astype(jnp.bfloat16)
    sums = jnp.dot(hit_near, msg_src, preferred_element_type=jnp.float32) + jnp.dot(
        hit_far, far_msgs, preferred_element_type=jnp.float32
    )
    counts = jnp.sum(hit_near.astype(jnp.float32), axis=1) + jnp.sum(
        hit_far.astype(jnp.float32), axis=1
    )
    sums, counts = lax.psum((sums, counts), "rep")
    unit_width = gru_bias.shape[1]
    start = lax.axis_index("rep") * unit_width
    state_part = lax.dynamic_slice_in_dim(memory, start, unit_width, 1)
    mean = sums / jnp.maximum(counts, 1.0)[:, None]
    highest = lax.Precision.HIGHEST
    a_parts = jnp.einsum("rk,gku->gru", mean, gru_input, precision=highest)
    b_parts = jnp.einsum("rk,gku->gru", memory, gru_hidden, precision=highest)
    update = jax.nn.sigmoid(a_parts[0] + b_parts[0] + gru_bias[0])
    reset = jax.nn.sigmoid(a_parts[1] + b_parts[1] + gru_bias[1])
    cand = jnp.tanh(a_parts[2] + gru_bias[2] + reset * (b_parts[2] + gru_bias[3]))
    fresh = (1.0 - update) * cand + update * state_part
    new_part = jnp.where((counts > 0.0)[:, None], fresh, state_part)
    updated = lax.all_gather(new_part.astype(jnp.bfloat16), "rep", axis=1, tiled=True)
    served = updated[jnp.maximum(got_nbr, 0)]
    returned = lax.all_to_all(served, "nodes", split_axis=0, concat_axis=0, tiled=True)
    fetched = returned.reshape(-1, updated.shape[1])[nbr_slot]
    kv_mem = jnp.dot(fetched, w_keyval_mem, preferred_element_type=jnp.float32).astype(jnp.bfloat16)
    kv_mem = lax.optimization_barrier(kv_mem).astype(jnp.float32)
    gaps = ticks[:, None] - nbr_tick.astype(jnp.float32)
    time_enc = encode(gaps, freq, phase).reshape(-1, freq.shape[0]).astype(jnp.bfloat16)
    kv_time = jnp.dot(time_enc, w_keyval_time, preferred_element_type=jnp.float32)
    keyval = (kv_mem + kv_time).reshape(events, neighbours, 2, HEADS, HEAD_DIM)
    query = jnp.dot(updated[src_local], w_query, preferred_element_type=jnp.float32).astype(
        jnp.bfloat16
    )
    query = lax.optimization_barrier(query).astype(jnp.float32).reshape(events, HEADS, HEAD_DIM)
    scores = jnp.einsum("ehd,ejhd->ehj", query, keyval[:, :, 0]) / math.sqrt(HEAD_DIM)
    weights = jax.nn.softmax(scores, axis=-1)
    mixed = jnp.einsum("ehj,ejhd->ehd", weights, keyval[:, :, 1])
    embed = mixed.reshape(events, HEADS * HEAD_DIM).astype(jnp.bfloat16)
    return (new_part, embed)


def on_device(
    memory,
    last_tick,
    src_local,
    dst_owner,
    dst_local,
    event_tick,
    nbr_owner,
    nbr_local,
    nbr_tick,
    freq,
    phase,
    w_message,
    gru_input,
    gru_hidden,
    gru_bias,
    w_query,
    w_keyval_mem,
    w_keyval_time,
):
    groups = lax.axis_size("nodes")
    rows_here = memory.shape[0]
    ticks = event_tick.astype(jnp.float32)
    cols = jnp.stack(
        [dst_owner[:, 0].astype(F32), dst_local.astype(F32), src_local.astype(F32), ticks], axis=1
    )
    new_part, new_half = update_rows(
        memory,
        last_tick.astype(F32)[:, None],
        cols,
        src_local[None, :],
        freq[None, :],
        phase[None, :],
        w_message,
        gru_input,
        gru_hidden,
        gru_bias,
        groups,
    )
    index = (nbr_owner[:, :, 0] * rows_here + nbr_local).astype(jnp.float32)
    gaps = ticks[:, None] - nbr_tick.astype(jnp.float32)
    embed = attend(
        new_half,
        src_local[:, None],
        index,
        gaps,
        freq[None, :],
        phase[None, :],
        w_query,
        w_keyval_mem,
        w_keyval_time,
        groups,
        lax.axis_size("rep"),
    )
    return (new_part, embed)


def solution(mesh):
    placed = (
        P("nodes", None),
        P("nodes"),
        P(("nodes", "rep")),
        P(("nodes", "rep"), None),
        P(("nodes", "rep")),
        P(("nodes", "rep")),
        P(("nodes", "rep"), None, None),
        P(("nodes", "rep"), None),
        P(("nodes", "rep"), None),
        P(),
        P(),
        P(),
        P(None, None, "rep"),
        P(None, None, "rep"),
        P(None, "rep"),
        P(),
        P(),
        P(),
    )
    fits = mesh.shape["nodes"] == 8 and mesh.shape["rep"] == 4
    return jax.shard_map(
        on_device if fits else on_device_large,
        mesh=mesh,
        in_specs=placed,
        out_specs=(P("nodes", "rep"), P(("nodes", "rep"), None)),
        check_vma=False,
    )
```
